128 devices in a mesh: dp: 8 (over x, core), tp: 16 (over z, y).
Axes of the slice: x: 4, y: 4, z: 4, core: 2. Of those that a mesh axis runs over, the one named last changes fastest.
Arguments:
- queries: bfloat16 [512, 3, 64, 576], P('dp', None, 'tp'), may hold values from -16 to 16
- latent_cache: bfloat16 [512, 128, 576], P('dp'), may hold values from -6 to 6
- new_latent: bfloat16 [512, 3, 576], P('dp'), may hold values from -6 to 6
- lengths: int32 [512], P('dp'), may hold values from 1 to 128, 32768 in all
- value_up_weight: bfloat16 [64, 512, 128], P('tp'), may hold values from -0.25 to 0.25
- out_proj: bfloat16 [8192, 7168], P('tp'), may hold values from -0.0625 to 0.0625
- residual: bfloat16 [512, 3, 7168], P('dp'), may hold values from -150 to 150
- norm_gain: float32 [7168], replicated, may hold values from 0.5 to 1.5
- head_weight: bfloat16 [7168, 65536], P(None, ('dp', 'tp'))
- mask_bits: int32 [512, 3, 128], P(None, None, ('dp', 'tp')), may hold values from 0 to 65535
- targets: int32 [512, 3], replicated, may hold values from 0 to 65535
Outputs:
- log_probs: float32 [512, 3, 65536], P(('dp', 'tp'))
- entropy: float32 [512, 3], P(('dp', 'tp'))
- row_loss: float32 [512], P(('dp', 'tp'))
The draws below stay inside these ranges and needn't reach their ends.
All inputs are finite; a program needn't handle non-finite values. No bound on the sum of `lengths` on one device may be relied on, other than what follows from the above.
Results may differ from the reference program's by a relative error of at most 0.02.
Values may be sent and summed in bfloat16 or wider, within the bound.
No kernel may reach another device: no remote copies, remote signals or barrier semaphores. Data moves between devices by JAX's collectives and lax.ppermute only.
A program may use at most 128 MiB of HBM per device.

```python
import math
import jax
import jax.numpy as jnp
import numpy as np
from jax import lax

D = 7168
H = 64
LAT = 512
KV = 576
VH = 128
VOCAB_DEV = 512
TILE = 32
STEPS = 3
CTX = 128
ROWS = 512
VOCAB = 65536
DEVICES = 128


def attention_signs(key):
    signs = jnp.where(jax.random.normal(key, (ROWS, KV)) >= 0.0, 1.0, -1.0)
    flips = jnp.where(jnp.arange(KV) < KV // 2, 1.0, -1.0)
    return (signs, signs * flips)


def head_direction(key):
    return jnp.where(jax.random.normal(key, (D,)) >= 0.0, 1.0, -1.0)


def draw_queries(key, part):
    first, second_operand = attention_signs(key)
    key = jax.random.fold_in(key, 1)
    base = jax.random.truncated_normal(key, -6.0, 6.0, (ROWS, STEPS, H, KV))
    unit = 6.0 * KV * 192.0 ** (-0.5)
    position = jnp.arange(STEPS).astype(jnp.float32)
    strong = (260.0 - 60.0 * position) / unit
    weaker = strong - 2.0 / unit
    aligned = strong[None, :, None] * first[:, None, :] + weaker[None, :, None] * second_operand[:, None, :]
    chosen = (jnp.arange(ROWS) % 8 == 1)[:, None, None, None]
    base = jnp.where(chosen, aligned[:, :, None, :], base)
    return base.astype(jnp.bfloat16)


def draw_latent_cache(key, part):
    first, second_operand = attention_signs(key)
    key = jax.random.fold_in(key, 2)
    base = jax.random.truncated_normal(key, -6.0, 6.0, (ROWS, CTX, KV))
    chosen = (jnp.arange(ROWS) % 8 == 1)[:, None, None] & (jnp.arange(CTX) == 0)[None, :, None]
    base = jnp.where(chosen, 6.0 * first[:, None, :], base)
    return base.astype(jnp.bfloat16)


def draw_new_latent(key, part):
    first, second_operand = attention_signs(key)
    key = jax.random.fold_in(key, 3)
    base = jax.random.truncated_normal(key, -6.0, 6.0, (ROWS, STEPS, KV))
    chosen = (jnp.arange(ROWS) % 8 == 1)[:, None, None] & (jnp.arange(STEPS) == 0)[None, :, None]
    base = jnp.where(chosen, 6.0 * second_operand[:, None, :], base)
    return base.astype(jnp.bfloat16)


def draw_residual(key, part):
    direction = head_direction(key)
    key = jax.random.fold_in(key, 4)
    key_noise, key_rows, key_cols = jax.random.split(key, 3)
    row_scale = 0.2 * jnp.exp(jax.random.uniform(key_rows, (ROWS, 1, 1), minval=0.0, maxval=math.log(10.0)))
    col_scale = jnp.exp(jax.random.uniform(key_cols, (1, 1, D), minval=math.log(0.3), maxval=math.log(3.0)))
    noise = jax.random.truncated_normal(key_noise, -6.0, 6.0, (ROWS, STEPS, D))
    base = noise * row_scale * col_scale
    cosine = 1.0 - 0.2 * jnp.arange(STEPS).astype(jnp.float32)
    sine = jnp.sqrt(1.0 - cosine * cosine)
    aligned = jnp.clip(50.0 * (cosine[None, :, None] * direction[None, None, :] + sine[None, :, None] * noise), -150.0, 150.0)
    chosen = (jnp.arange(ROWS) % 16 == 3)[:, None, None]
    base = jnp.where(chosen, aligned, base)
    return base.astype(jnp.bfloat16)


def draw_head_weight(key, part):
    direction = head_direction(key)
    key = jax.random.fold_in(key, 5)
    key_noise, key_cols = jax.random.split(key, 2)
    columns = jnp.arange(VOCAB).astype(jnp.float32)
    col_scale = 0.5 / math.sqrt(D) * jnp.exp(jax.random.uniform(key_cols, (1, VOCAB), minval=0.0, maxval=math.log(10.0))) * jnp.power(3.0, columns / VOCAB)[None, :]
    base = jax.random.truncated_normal(key_noise, -6.0, 6.0, (D, VOCAB)) * col_scale
    base = base.at[:, 0].set(300.0 * direction / D)
    base = base.at[:, VOCAB // 2 + 5].set(302.25 * direction / D)
    return base.astype(jnp.bfloat16)


def place_ends(result, rng, smallest, largest):
    spot = [jax.random.randint(jax.random.fold_in(rng, axis), (), 0, length) for axis, length in enumerate(result.shape)]
    longest = result.shape.index(max(result.shape))
    beside = spot[:longest] + [(spot[longest] + 1) % result.shape[longest]] + spot[longest + 1:]
    return result.at[tuple(spot)].set(smallest).at[tuple(beside)].set(largest)


def level_of(own_key, shape, shards, low, top_value):
    def one(dim, shards_of):
        draws = jax.random.uniform(jax.random.fold_in(jax.random.fold_in(own_key, 6), dim), (shards_of,), jnp.float32, low / len(shards), top_value / len(shards))
        return jnp.repeat(jnp.exp(draws), shape[dim] // shards_of).reshape((-1,) + (1,) * (len(shape) - dim - 1))

    loudness = one(*shards[0])
    for cut in shards[1:]:
        loudness = loudness * one(*cut)
    return loudness


def profile(count, total, limit, skew):
    weights = [(1 << 20) // math.isqrt(rank ** skew) + 1 for rank in range(2, count + 1)]
    rest, counts = total - limit - (count - 1), [1] * (count - 1)
    while rest > 0:
        free = [i for i in range(count - 1) if counts[i] < limit]
        mass, budget = sum([weights[i] for i in free]), rest
        for i in free:
            more = min(limit - counts[i], max(1, budget * weights[i] // mass), rest)
            counts[i] = counts[i] + more
            rest = rest - more
    return np.array([limit] + counts)


def uneven_parts(rng, number_of, total, most, slope):
    if number_of == 2:
        one = jax.random.randint(rng, (), max(1, total - most), min(most, total - 1) + 1)
        return jnp.stack([one, total - one])
    tallies = jnp.asarray(profile(number_of, total, most, slope), jnp.int32)
    twos = (number_of - 1) // 2
    giver, taker = tallies[1:1 + 2 * twos:2], tallies[2:2 + 2 * twos:2]
    room = jnp.minimum(giver - 1, most - taker)
    moved = jax.random.randint(jax.random.fold_in(rng, 1), (twos,), 0, 1 << 20) % (room + 1)
    tallies = tallies.at[1:1 + 2 * twos:2].set(giver - moved).at[2:2 + 2 * twos:2].set(taker + moved)
    return tallies[jax.random.permutation(jax.random.fold_in(rng, 2), number_of)]


def centred(own_key, extent, width, bound, pieces=(), kind=jnp.bfloat16):
    entries = width * jax.random.normal(own_key, extent, jnp.float32)
    if pieces:
        entries = entries * level_of(own_key, extent, pieces, -0.22, 0.18)
    return jnp.clip(entries, -bound, bound).astype(kind)


def setup_inputs(seed: int = 0) -> dict:
    key_of = jax.random.split(jax.random.key(seed), 12)
    return {
        "queries": draw_queries(jax.random.fold_in(key_of[11], 71), 0),
        "latent_cache": draw_latent_cache(jax.random.fold_in(key_of[11], 71), 0),
        "new_latent": draw_new_latent(jax.random.fold_in(key_of[11], 71), 0),
        "lengths": uneven_parts(key_of[3], ROWS, ROWS * CTX // 2, CTX, 2).astype(jnp.int32),
        "value_up_weight": centred(key_of[4], (H, LAT, VH), LAT ** -0.5, 0.25, ((0, 16),)),
        "out_proj": centred(key_of[5], (H * VH, D), (H * VH) ** -0.5, 0.0625, ((0, 16),)),
        "residual": draw_residual(jax.random.fold_in(key_of[11], 71), 0),
        "norm_gain": jnp.clip(1.0 + 0.1 * jax.random.normal(key_of[7], (D,), jnp.float32), 0.5, 1.5),
        "head_weight": draw_head_weight(jax.random.fold_in(key_of[11], 71), 0),
        "mask_bits": place_ends(jax.random.randint(key_of[9], (ROWS, STEPS, DEVICES), 0, 65536), jax.random.fold_in(key_of[9], 1), 0, 65535).astype(jnp.int32),
        "targets": place_ends(jax.random.randint(key_of[10], (ROWS, STEPS), 0, VOCAB), jax.random.fold_in(key_of[10], 1), 0, VOCAB - 1).astype(jnp.int32),
    }


score_scale = 192.0 ** (-0.5)
neg_large = -1e+30

def reference(queries, latent_cache, new_latent, lengths, value_up_weight, out_proj, residual, norm_gain, head_weight, mask_bits, targets):
    query_f = queries.astype(jnp.float32)
    cache_f = latent_cache.astype(jnp.float32)
    fresh_f = new_latent.astype(jnp.float32)
    cache_scores = jnp.einsum('rshk,rpk->rshp', query_f, cache_f) * score_scale
    new_scores = jnp.einsum('rshk,rjk->rshj', query_f, fresh_f) * score_scale
    valid_cache = (jnp.arange(CTX, dtype=jnp.int32)[None, :] < lengths[:, None])[:, None, None, :]
    valid_new = (jnp.arange(STEPS, dtype=jnp.int32)[None, :] <= jnp.arange(STEPS, dtype=jnp.int32)[:, None])[None, :, None, :]
    top_score = jnp.maximum(lax.optimization_barrier(jnp.max(jnp.where(valid_cache, cache_scores, neg_large), axis=-1)), lax.optimization_barrier(jnp.max(jnp.where(valid_new, new_scores, neg_large), axis=-1)))[..., None]
    cache_exp = jnp.where(valid_cache, jnp.exp(cache_scores - top_score), 0.0)
    new_exp = jnp.where(valid_new, jnp.exp(new_scores - top_score), 0.0)
    denom = lax.optimization_barrier(jnp.sum(cache_exp, axis=-1, keepdims=True)) + lax.optimization_barrier(jnp.sum(new_exp, axis=-1, keepdims=True))
    cache_probs = (cache_exp / denom).astype(jnp.bfloat16).astype(jnp.float32)
    new_probs = (new_exp / denom).astype(jnp.bfloat16).astype(jnp.float32)
    latent_result_rows = (jnp.einsum('rshp,rpk->rshk', cache_probs, cache_f[:, :, :LAT]) + jnp.einsum('rshj,rjk->rshk', new_probs, fresh_f[:, :, :LAT])).astype(jnp.bfloat16)
    per_head_value_rows = jnp.einsum('cezq,zql->cezl', latent_result_rows.astype(jnp.float32), value_up_weight.astype(jnp.float32))
    per_head_value_rows = per_head_value_rows.astype(jnp.bfloat16).reshape(ROWS, STEPS, H * VH)
    attn_out = jnp.dot(per_head_value_rows, out_proj, preferred_element_type=jnp.float32)
    summed = residual.astype(jnp.float32) + attn_out
    mean_square = lax.optimization_barrier(jnp.mean(summed * summed, axis=-1, keepdims=True))
    hidden = (summed * lax.rsqrt(mean_square + 1e-06) * norm_gain).astype(jnp.bfloat16)
    logits = jnp.dot(hidden, head_weight, preferred_element_type=jnp.float32)
    vocab_index = jnp.arange(VOCAB, dtype=jnp.int32)
    owner = vocab_index // VOCAB_DEV
    tile_bit = vocab_index % VOCAB_DEV // TILE
    words = mask_bits[:, :, owner]
    bit_set = jnp.bitwise_and(jnp.right_shift(words, tile_bit[None, None, :]), 1) == 1
    is_target = vocab_index[None, None, :] == targets[:, :, None]
    allowed = jnp.logical_or(bit_set, is_target)
    peak = lax.optimization_barrier(jnp.max(jnp.where(allowed, logits, neg_large), axis=-1))
    shifted = logits - peak[..., None]
    weights = jnp.where(allowed, jnp.exp(shifted), 0.0)
    total = lax.optimization_barrier(jnp.sum(weights, axis=-1))
    moment = lax.optimization_barrier(jnp.sum(weights * shifted, axis=-1))
    target_logit = lax.optimization_barrier(jnp.sum(jnp.where(is_target, logits, 0.0), axis=-1))
    log_partition_sum = peak + jnp.log(total)
    log_probs = jnp.where(allowed, logits - log_partition_sum[..., None], 0.0)
    entropy = jnp.log(total) - moment / total
    row_loss = lax.optimization_barrier(jnp.mean(log_partition_sum - target_logit, axis=1))
    return (log_probs, entropy, row_loss)
```

```python
import jax
import jax.numpy as jnp
from jax import lax
from jax.sharding import PartitionSpec as P

LAT = 512


score_scale = 192.0 ** (-0.5)
neg_large = -1e30


def normalize(resid_rows, attn_rows, norm_gain):
    summed = resid_rows.astype(jnp.float32) + attn_rows
    mean_square = jnp.mean(summed * summed, axis=-1, keepdims=True)
    return (summed * lax.rsqrt(mean_square + 1e-06) * norm_gain).astype(jnp.bfloat16)


def attention(queries, latent_cache, new_latent, lengths, value_up_weight):
    group_rows_count, steps_count = (queries.shape[0], queries.shape[1])
    context = latent_cache.shape[1]
    cache_scores = (
        jnp.einsum("rshk,rpk->rshp", queries, latent_cache, preferred_element_type=jnp.float32)
        * score_scale
    )
    new_scores = (
        jnp.einsum("rshk,rjk->rshj", queries, new_latent, preferred_element_type=jnp.float32)
        * score_scale
    )
    valid_cache = (lax.iota(jnp.int32, context)[None, :] < lengths[:, None])[:, None, None, :]
    position = lax.iota(jnp.int32, steps_count)
    valid_new = (position[None, :] <= position[:, None])[None, :, None, :]
    top_score = jnp.maximum(
        jnp.max(jnp.where(valid_cache, cache_scores, neg_large), axis=-1),
        jnp.max(jnp.where(valid_new, new_scores, neg_large), axis=-1),
    )[..., None]
    cache_exp = jnp.where(valid_cache, jnp.exp(cache_scores - top_score), 0.0)
    new_exp = jnp.where(valid_new, jnp.exp(new_scores - top_score), 0.0)
    denom = jnp.sum(cache_exp, axis=-1, keepdims=True) + jnp.sum(new_exp, axis=-1, keepdims=True)
    cache_probs = (cache_exp / denom).astype(jnp.bfloat16)
    new_probs = (new_exp / denom).astype(jnp.bfloat16)
    latent_result_rows = (
        jnp.einsum(
            "rshp,rpk->rshk",
            cache_probs,
            latent_cache[:, :, :LAT],
            preferred_element_type=jnp.float32,
        )
        + jnp.einsum(
            "rshj,rjk->rshk", new_probs, new_latent[:, :, :LAT], preferred_element_type=jnp.float32
        )
    ).astype(jnp.bfloat16)
    per_head_value_rows = jnp.einsum(
        "cezq,zql->cezl", latent_result_rows, value_up_weight, preferred_element_type=jnp.float32
    ).astype(jnp.bfloat16)
    return per_head_value_rows.reshape(group_rows_count, steps_count, -1)


def body(
    queries,
    latent_cache,
    new_latent,
    lengths,
    value_up_weight,
    out_proj,
    residual,
    norm_gain,
    head_weight,
    mask_bits,
    targets,
):
    per_head_value_rows = attention(queries, latent_cache, new_latent, lengths, value_up_weight)
    tp_count = lax.axis_size("tp")
    owned_row_block = queries.shape[0] // tp_count
    partial = jnp.dot(
        per_head_value_rows, out_proj, preferred_element_type=jnp.float32
    ).astype(jnp.bfloat16)
    partial = partial.reshape((tp_count, owned_row_block) + partial.shape[1:])
    partial = lax.all_to_all(partial, "tp", split_axis=0, concat_axis=0, tiled=True)
    attn_rows = jnp.sum(partial.astype(jnp.float32), axis=0)
    resid_rows = lax.dynamic_slice_in_dim(
        residual, lax.axis_index("tp") * owned_row_block, owned_row_block, 0
    )
    hidden = normalize(resid_rows, attn_rows, norm_gain)
    logits = jnp.dot(
        lax.all_gather(hidden, ("dp", "tp"), axis=0, tiled=True),
        head_weight,
        preferred_element_type=jnp.float32,
    )
    vocab_dev = head_weight.shape[1]
    devices_all = lax.axis_size("dp") * lax.axis_size("tp")
    device_id = lax.axis_index("dp") * lax.axis_size("tp") + lax.axis_index("tp")
    columns = lax.iota(jnp.int32, vocab_dev)
    tile_bit = columns // (vocab_dev // 16)
    bit_set = jnp.bitwise_and(jnp.right_shift(mask_bits, tile_bit[None, None, :]), 1) == 1
    local_target = targets - device_id * vocab_dev
    is_target = columns[None, None, :] == local_target[:, :, None]
    allowed = jnp.logical_or(bit_set, is_target)
    masked = jnp.where(allowed, logits, neg_large)
    part_target = jnp.sum(jnp.where(is_target, logits, 0.0), axis=-1)
    part_peak = jnp.max(masked, axis=-1)
    shifted = logits - part_peak[..., None]
    weights = jnp.where(allowed, jnp.exp(shifted), 0.0)
    part_total = jnp.sum(weights, axis=-1)
    part_moment = jnp.sum(weights * shifted, axis=-1)
    sent = jnp.where(allowed, shifted, 1.0).astype(jnp.bfloat16)
    stats = jnp.stack([part_peak, part_total, part_moment, part_target], axis=0)
    rows_per_device = logits.shape[0] // devices_all
    steps = logits.shape[1]
    stats = stats.reshape(4, devices_all, rows_per_device, steps).transpose(1, 0, 2, 3)
    stats = lax.all_to_all(
        stats.reshape(devices_all, -1), ("dp", "tp"), split_axis=0, concat_axis=0, tiled=True
    ).reshape(devices_all, 4, rows_per_device, steps)
    owned = lax.all_to_all(
        sent.reshape(devices_all, rows_per_device, steps, vocab_dev),
        ("dp", "tp"),
        split_axis=0,
        concat_axis=0,
        tiled=True,
    ).astype(jnp.float32)
    peaks, totals, moments, target_parts = (stats[:, i] for i in range(4))
    peak = jnp.max(peaks, axis=0)
    lift = peaks - peak
    scale = jnp.exp(lift)
    total = jnp.sum(scale * totals, axis=0)
    moment = jnp.sum(scale * (moments + lift * totals), axis=0)
    target_logit = jnp.sum(target_parts, axis=0)
    log_partition_sum = peak + jnp.log(total)
    log_probs = jnp.where(owned > 0.0, 0.0, owned + (peaks - log_partition_sum)[..., None])
    log_probs = log_probs.transpose(1, 2, 0, 3).reshape(rows_per_device, steps, -1)
    entropy = jnp.log(total) - moment / total
    row_loss = jnp.mean(log_partition_sum - target_logit, axis=1)
    return (log_probs, entropy, row_loss)


def solution(mesh):
    placed = (
        P("dp", None, "tp", None),
        P("dp", None, None),
        P("dp", None, None),
        P("dp"),
        P("tp", None, None),
        P("tp", None),
        P("dp", None, None),
        P(),
        P(None, ("dp", "tp")),
        P(None, None, ("dp", "tp")),
        P(),
    )
    return jax.shard_map(
        body,
        mesh=mesh,
        in_specs=placed,
        out_specs=(P(("dp", "tp"), None, None), P(("dp", "tp"), None), P(("dp", "tp"))),
        check_vma=False,
    )
```

```python
import jax
import jax.numpy as jnp
from jax import lax
from jax.sharding import PartitionSpec as P

LAT = 512
TP = ("z", "y")
SAME = ("x", "z", "y")


score_scale = 192.0 ** (-0.5)
neg_large = -1e30


def attention(queries, latent_cache, new_latent, lengths, value_up_weight):
    group_rows_count, steps_count = (queries.shape[0], queries.shape[1])
    context = latent_cache.shape[1]
    cache_scores = (
        jnp.einsum("rshk,rpk->rshp", queries, latent_cache, preferred_element_type=jnp.float32)
        * score_scale
    )
    new_scores = (
        jnp.einsum("rshk,rjk->rshj", queries, new_latent, preferred_element_type=jnp.float32)
        * score_scale
    )
    valid_cache = (lax.iota(jnp.int32, context)[None, :] < lengths[:, None])[:, None, None, :]
    position = lax.iota(jnp.int32, steps_count)
    valid_new = (position[None, :] <= position[:, None])[None, :, None, :]
    top_score = jnp.maximum(
        jnp.max(jnp.where(valid_cache, cache_scores, neg_large), axis=-1),
        jnp.max(jnp.where(valid_new, new_scores, neg_large), axis=-1),
    )[..., None]
    cache_exp = jnp.where(valid_cache, jnp.exp(cache_scores - top_score), 0.0)
    new_exp = jnp.where(valid_new, jnp.exp(new_scores - top_score), 0.0)
    denom = jnp.sum(cache_exp, axis=-1, keepdims=True) + jnp.sum(new_exp, axis=-1, keepdims=True)
    cache_probs = (cache_exp / denom).astype(jnp.bfloat16)
    new_probs = (new_exp / denom).astype(jnp.bfloat16)
    latent_result_rows = (
        jnp.einsum(
            "rshp,rpk->rshk",
            cache_probs,
            latent_cache[:, :, :LAT],
            preferred_element_type=jnp.float32,
        )
        + jnp.einsum(
            "rshj,rjk->rshk", new_probs, new_latent[:, :, :LAT], preferred_element_type=jnp.float32
        )
    ).astype(jnp.bfloat16)
    per_head_value_rows = jnp.einsum(
        "cezq,zql->cezl", latent_result_rows, value_up_weight, preferred_element_type=jnp.float32
    ).astype(jnp.bfloat16)
    return per_head_value_rows.reshape(group_rows_count, steps_count, -1)


def body(
    queries,
    latent_cache,
    new_latent,
    lengths,
    value_up_weight,
    out_proj,
    residual,
    norm_gain,
    head_weight,
    mask_bits,
    targets,
):
    rows, steps = queries.shape[:2]
    width = residual.shape[2]
    half = width // 2
    vocab_dev = head_weight.shape[1]
    x_count, cores, tp_count = lax.axis_size("x"), lax.axis_size("core"), lax.axis_size(TP)
    core, tp = lax.axis_index("core"), lax.axis_index(TP)
    groups = tp_count // 2
    group_rows = rows // groups
    pairs = steps * group_rows
    weights_pair = lax.all_gather(head_weight, "core", axis=0)

    def of_core(full, which):
        cut = full.reshape(x_count, cores, groups, group_rows, steps)
        cut = lax.dynamic_index_in_dim(cut, which, 1, keepdims=False)
        return cut.transpose(0, 1, 3, 2).reshape(-1)

    words_own = of_core(mask_bits, core)
    words_other = lax.ppermute(of_core(mask_bits, 1 - core), "core", ((0, 1), (1, 0)))
    words = jnp.where(core == 0, jnp.stack([words_own, words_other]), jnp.stack([words_other, words_own]))
    row_targets = of_core(targets, core)

    values = attention(queries, latent_cache, new_latent, lengths, value_up_weight)
    values = values.reshape(groups, group_rows, steps, -1).transpose(0, 2, 1, 3)
    values = values.reshape(groups * pairs, -1)
    partial = jnp.stack(
        [
            jnp.dot(values, out_proj[:, :half], preferred_element_type=jnp.float32),
            jnp.dot(values, out_proj[:, half:], preferred_element_type=jnp.float32),
        ]
    ).astype(jnp.bfloat16)
    partial = lax.all_to_all(
        partial.reshape(tp_count, pairs, half), TP, split_axis=0, concat_axis=0, tiled=True
    )
    partial, weights_pair = lax.optimization_barrier((partial, weights_pair))
    own_half, own_group = tp // groups, tp % groups
    resid = lax.dynamic_slice(
        residual.transpose(1, 0, 2),
        (0, own_group * group_rows, own_half * half),
        (steps, group_rows, half),
    ).reshape(pairs, half)
    gain = lax.dynamic_slice_in_dim(norm_gain, own_half * half, half, 0)
    summed = resid.astype(jnp.float32) + jnp.sum(partial.astype(jnp.float32), axis=0)
    squares = jnp.sum(summed * summed, axis=-1)
    hidden = (summed * gain).astype(jnp.bfloat16)
    hidden = lax.all_gather(hidden, SAME, axis=0).reshape(x_count, 2, groups * pairs, half)
    squares = lax.all_gather(squares, SAME, axis=0).reshape(x_count, 2, groups * pairs)
    norm = lax.rsqrt(jnp.sum(squares, axis=1) / width + 1e-06).reshape(-1)

    columns = lax.iota(jnp.int32, vocab_dev)
    tile_bit = columns // (vocab_dev // 16)
    shifted_by_core, allowed_by_core, target_parts, masked_peaks = [], [], [], []
    for which in range(cores):
        weight = weights_pair[which]
        logits = jnp.dot(
            hidden[:, 0].reshape(-1, half), weight[:half], preferred_element_type=jnp.float32
        ) + jnp.dot(
            hidden[:, 1].reshape(-1, half), weight[half:], preferred_element_type=jnp.float32
        )
        logits = logits * norm[:, None]
        shard = (lax.axis_index("x") * cores + which) * tp_count + tp
        bit_set = jnp.bitwise_and(jnp.right_shift(words[which][:, None], tile_bit[None, :]), 1) == 1
        is_target = columns[None, :] == (row_targets - shard * vocab_dev)[:, None]
        allowed = jnp.logical_or(bit_set, is_target)
        shifted_by_core.append(logits)
        allowed_by_core.append(allowed)
        target_parts.append(jnp.sum(jnp.where(is_target, logits, 0.0), axis=-1))
        masked_peaks.append(jnp.max(jnp.where(allowed, logits, neg_large), axis=-1))
    part_peak = jnp.maximum(*masked_peaks)
    part_total, part_moment, sent = 0.0, 0.0, []
    for which in range(cores):
        shifted = shifted_by_core[which] - part_peak[:, None]
        weight = jnp.where(allowed_by_core[which], jnp.exp(shifted), 0.0)
        part_total = part_total + jnp.sum(weight, axis=-1)
        part_moment = part_moment + jnp.sum(weight * shifted, axis=-1)
        sent.append(jnp.where(allowed_by_core[which], shifted, 1.0).astype(jnp.bfloat16))
    stats = jnp.stack([part_peak, part_total, part_moment, target_parts[0] + target_parts[1]])
    stats = lax.all_gather(stats, SAME, axis=0)
    own_rows = rows // tp_count
    spread = (x_count, groups, steps, group_rows // own_rows, own_rows)
    sent = jnp.stack([one.reshape(spread + (vocab_dev,)) for one in sent], axis=4)
    sent = sent.transpose(0, 1, 3, 2, 4, 5, 6)
    sent = sent.reshape(x_count * tp_count, steps * cores * own_rows, vocab_dev)
    owned = lax.all_to_all(sent, SAME, split_axis=0, concat_axis=0, tiled=True)
    owned = owned.reshape(x_count, tp_count, steps, cores, own_rows, vocab_dev)

    stats = lax.dynamic_slice(
        stats.reshape((x_count * tp_count, 4) + spread),
        (0, 0, lax.axis_index("x"), tp // 2, 0, tp % 2, 0),
        (x_count * tp_count, 4, 1, 1, steps, 1, own_rows),
    ).reshape(x_count, tp_count, 4, steps, own_rows)
    peaks, totals, moments, target_part = (stats[:, :, i] for i in range(4))
    peak = jnp.max(peaks, axis=(0, 1))
    lift = peaks - peak
    scale = jnp.exp(lift)
    total = jnp.sum(scale * totals, axis=(0, 1))
    moment = jnp.sum(scale * (moments + lift * totals), axis=(0, 1))
    target_logit = jnp.sum(target_part, axis=(0, 1))
    log_partition_sum = peak + jnp.log(total)
    offset = (peaks - log_partition_sum)[:, :, :, None, :, None]
    owned = owned.astype(jnp.float32)
    log_probs = jnp.where(owned > 0.0, 0.0, owned + offset)
    log_probs = log_probs.transpose(4, 2, 0, 3, 1, 5).reshape(own_rows, steps, -1)
    entropy = (jnp.log(total) - moment / total).T
    row_loss = jnp.mean(log_partition_sum - target_logit, axis=0)
    return (log_probs, entropy, row_loss)


def solution(mesh):
    mesh = jax.sharding.Mesh(mesh.devices.reshape(4, 2, 4, 4), ("x", "core", "z", "y"))
    dp, all_axes = ("x", "core"), ("x", "core", "z", "y")
    placed = (
        P(dp, None, TP, None),
        P(dp, None, None),
        P(dp, None, None),
        P(dp),
        P(TP, None, None),
        P(TP, None),
        P(dp, None, None),
        P(),
        P(None, all_axes),
        P(None, None, all_axes),
        P(),
    )
    return jax.shard_map(
        body,
        mesh=mesh,
        in_specs=placed,
        out_specs=(P(all_axes, None, None), P(all_axes, None), P(all_axes)),
        check_vma=False,
    )
```

```python
import functools

import jax
import jax.numpy as jnp
from jax import lax
from jax.experimental import pallas as pl
from jax.experimental.pallas import tpu as pltpu
from jax.sharding import PartitionSpec as P

LAT = 512
DP = ("xh", "xl", "core")
TP = ("z", "y")


score_scale = 192.0 ** (-0.5)
neg_large = -1e30


def attend(lengths, queries_ref, cache_ref, new_ref, up_ref, start, count):
    context = cache_ref.shape[2]
    steps, heads = queries_ref.shape[1:3]
    value = up_ref.shape[2]
    tall = count * 16
    position = lax.broadcasted_iota(jnp.int32, (1, context), 1)
    blank = jnp.zeros((heads, queries_ref.shape[3]), jnp.float32)
    lines = []
    for row in range(start, start + count):
        parts = [queries_ref[row, step].astype(jnp.float32) for step in range(steps)]
        lines.append(jnp.concatenate(parts + [blank], axis=0).astype(jnp.bfloat16))
    latents = jnp.concatenate(
        [new_ref[place].astype(jnp.float32)[start : start + count] for place in range(steps)], axis=0
    ).astype(jnp.bfloat16)
    scores = []
    for row in range(count):
        one = jnp.dot(lines[row], cache_ref[start + row], preferred_element_type=jnp.float32)
        scores.append(jnp.where(position < lengths[row], one * score_scale, neg_large))
    scores = jnp.concatenate(scores, axis=0)
    fresh = lax.dot_general(
        jnp.concatenate(lines, axis=0),
        latents,
        (((1,), (1,)), ((), ())),
        preferred_element_type=jnp.float32,
    )
    line = lax.broadcasted_iota(jnp.int32, fresh.shape, 0)
    key = lax.broadcasted_iota(jnp.int32, fresh.shape, 1)
    step = (line % 16) // 4
    own = jnp.logical_and(line // 16 == key % count, key // count <= step)
    fresh = jnp.where(own, fresh * score_scale, neg_large)
    top = jnp.maximum(
        jnp.max(scores, axis=1, keepdims=True), jnp.max(fresh, axis=1, keepdims=True)
    )
    scores = jnp.exp(scores - top)
    fresh = jnp.exp(fresh - top)
    denom = jnp.sum(scores, axis=1, keepdims=True) + jnp.sum(fresh, axis=1, keepdims=True)
    scores = (scores / denom).astype(jnp.bfloat16)
    fresh = (fresh / denom).astype(jnp.bfloat16)
    latent = []
    for row in range(count):
        latent.append(
            lax.dot_general(
                scores[row * 16 : row * 16 + 16],
                cache_ref[start + row, :LAT, :],
                (((1,), (1,)), ((), ())),
                preferred_element_type=jnp.float32,
            )
        )
    latent = jnp.concatenate(latent, axis=0) + jnp.dot(
        fresh, latents[:, :LAT], preferred_element_type=jnp.float32
    )
    latent = latent.astype(jnp.bfloat16)
    values = jnp.concatenate(
        [jnp.dot(latent, up_ref[head], preferred_element_type=jnp.float32) for head in range(heads)],
        axis=1,
    )
    line = lax.broadcasted_iota(jnp.int32, values.shape, 0)
    entry = lax.broadcasted_iota(jnp.int32, values.shape, 1)
    values = jnp.where(line % 4 == entry // value, values, 0.0).astype(jnp.bfloat16)
    shape = (steps * count, tall)
    target = lax.broadcasted_iota(jnp.int32, shape, 0)
    line = lax.broadcasted_iota(jnp.int32, shape, 1)
    pick = jnp.logical_and(target % count == line // 16, target // count == (line % 16) // 4)
    pick = jnp.where(pick, 1.0, 0.0).astype(jnp.bfloat16)
    return jnp.dot(pick, values, preferred_element_type=jnp.float32)


def attention_kernel(
    lengths_ref, queries_ref, cache_ref, new_ref, up_ref, project_ref, out_ref, values_ref, weight_ref, sems
):
    g = pl.program_id(0)
    parts = sems.shape[0]
    depth = weight_ref.shape[0] // parts
    copies = [
        pltpu.make_async_copy(
            project_ref.at[pl.ds(part * depth, depth)],
            weight_ref.at[pl.ds(part * depth, depth)],
            sems.at[part],
        )
        for part in range(parts)
    ]

    @pl.when(g == 0)
    def _():
        for copy in copies:
            copy.start()

    count = 8
    block = cache_ref.shape[0]
    lengths = [lengths_ref[g * block + row] for row in range(block)]
    values = [
        attend(lengths[start : start + count], queries_ref, cache_ref, new_ref, up_ref, start, count)
        for start in range(0, block, count)
    ]
    values = jnp.concatenate(values, axis=0).astype(jnp.bfloat16)
    lines = values.shape[0]
    values_ref[pl.ds(pl.multiple_of(g * lines, lines), lines), :] = values

    @pl.when(g == pl.num_programs(0) - 1)
    def _():
        for copy in copies:
            copy.wait()
        half = out_ref.shape[2]
        cut = half // 4
        for part in range(8):
            columns = slice((part % 4) * cut, (part % 4 + 1) * cut)
            out_ref[part // 4, :, columns] = jnp.dot(
                values_ref[...],
                weight_ref[:, part * cut : (part + 1) * cut],
                preferred_element_type=jnp.float32,
            ).astype(jnp.bfloat16)


def attention(queries, latent_cache, new_latent, lengths, value_up_weight, out_proj):
    rows, steps, heads, entries = queries.shape
    context = latent_cache.shape[1]
    block = 16
    depth, width = out_proj.shape
    return pl.pallas_call(
        attention_kernel,
        grid_spec=pltpu.PrefetchScalarGridSpec(
            num_scalar_prefetch=1,
            grid=(rows // block,),
            in_specs=[
                pl.BlockSpec((block, steps, heads, entries), lambda g, _: (g, 0, 0, 0)),
                pl.BlockSpec((block, entries, context), lambda g, _: (g, 0, 0)),
                pl.BlockSpec((steps, block, entries), lambda g, _: (0, g, 0)),
                pl.BlockSpec(value_up_weight.shape, lambda g, _: (0, 0, 0)),
                pl.BlockSpec(memory_space=pl.ANY),
            ],
            out_specs=pl.BlockSpec((2, rows * steps, width // 2), lambda g, _: (0, 0, 0)),
            scratch_shapes=[
                pltpu.VMEM((rows * steps, depth), jnp.bfloat16),
                pltpu.VMEM((depth, width), jnp.bfloat16),
                pltpu.SemaphoreType.DMA((4,)),
            ],
        ),
        out_shape=jax.ShapeDtypeStruct((2, rows * steps, width // 2), jnp.bfloat16),
        compiler_params=pltpu.CompilerParams(vmem_limit_bytes=56 * 1024 * 1024),
        cost_estimate=pl.CostEstimate(
            flops=4 * rows * 16 * context * entries + 2 * rows * steps * depth * width,
            bytes_accessed=2 * rows * context * entries + 2 * depth * width,
            transcendentals=rows * 16 * context,
        ),
        name="latent_attention",
    )(
        lengths,
        queries,
        latent_cache.transpose(0, 2, 1),
        new_latent.transpose(1, 0, 2),
        value_up_weight,
        out_proj,
    )


def head_kernel(steps, per_block, k_blocks, width, a_ref, *refs):
    weight_refs = refs[:4]
    meta_ref, gain_ref, out_ref, acc_ref, squares_ref = refs[4:]
    k = pl.program_id(0)

    @pl.when(k == 0)
    def _():
        acc_ref[...] = jnp.zeros_like(acc_ref)
        squares_ref[...] = jnp.zeros_like(squares_ref)

    rows, depth = a_ref.shape[1:]
    vocab = weight_refs[0].shape[1]
    a = a_ref[0]
    for shard, weight_ref in enumerate(weight_refs):
        acc_ref[shard] += jnp.dot(a, weight_ref[...], preferred_element_type=jnp.float32)
    inverse = 1.0 / gain_ref[...]
    wide = a.astype(jnp.float32) * inverse
    wide = wide * wide
    part = wide[:, :128]
    for lane in range(128, depth, 128):
        part = part + wide[:, lane : lane + 128]
    squares_ref[...] += part

    @pl.when(k == k_blocks - 1)
    def _():
        column = lax.broadcasted_iota(jnp.int32, (1, vocab), 1)
        bit = column // (vocab // 16)
        lane = lax.broadcasted_iota(jnp.int32, (1, 128), 1)
        upper = lax.broadcasted_iota(jnp.int32, (1, 8, 1), 1) < 4

        def of_step(full, step):
            return full.reshape(-1, steps, 8, full.shape[1])[:, step]

        def by_owner(first, second):
            count = first.shape[2]
            low = jnp.where(upper, first, pltpu.roll(second, 4, 1))
            high = jnp.where(upper, pltpu.roll(first, 4, 1), second)
            low, high = (one.reshape(-1, 2, 8, count) for one in (low, high))
            return jnp.stack([low, high], axis=1).reshape(-1, count).astype(jnp.bfloat16)

        for block in range(rows // per_block):
            own = pl.ds(block * per_block, per_block)
            to = pl.ds(block * (per_block // steps * 2), per_block // steps * 2)
            square = jnp.sum(squares_ref[own, :], axis=1, keepdims=True)
            norm = lax.rsqrt(square * (1.0 / width) + 1e-06)
            logits, allowed, target, peak = [], [], 0.0, neg_large
            for shard in range(4):
                one = acc_ref[shard, own, :] * norm
                word = meta_ref[shard, own, :]
                is_target = column == meta_ref[4 + shard, own, :]
                open_bit = jnp.bitwise_and(jnp.right_shift(word, bit), 1) == 1
                ok = jnp.logical_or(open_bit, is_target)
                logits.append(one)
                allowed.append(ok)
                target = target + jnp.where(is_target, one, 0.0)
                peak = jnp.maximum(peak, jnp.where(ok, one, neg_large))
            target = jnp.sum(target, axis=1, keepdims=True)
            peak = jnp.max(peak, axis=1, keepdims=True)
            total, moment, sent = 0.0, 0.0, []
            for ok, one in zip(allowed, logits):
                shifted = jnp.where(ok, one - peak, 0.0)
                weight = jnp.where(ok, jnp.exp(shifted), 0.0)
                total = total + weight
                moment = moment + weight * shifted
                sent.append(jnp.where(ok, shifted, 1.0))
            total = jnp.sum(total, axis=1, keepdims=True)
            moment = jnp.sum(moment, axis=1, keepdims=True)
            packed = jnp.zeros((per_block, 128), jnp.float32)
            lanes = 0
            for stat, count in ((peak, 3), (total, 2), (moment, 2), (target, 3)):
                for _ in range(count):
                    piece = stat.astype(jnp.bfloat16).astype(jnp.float32)
                    packed = jnp.where(lane == lanes, piece, packed)
                    stat = stat - piece
                    lanes += 1
            sums = 0.0
            for step in range(steps):
                for two in range(2):
                    start = (step * 2 + two) * vocab
                    out_ref[to, start : start + vocab] = by_owner(
                        of_step(sent[2 * two], step), of_step(sent[2 * two + 1], step)
                    )
                mine = of_step(packed, step)
                sums = sums + (pltpu.roll(mine, step * lanes, 2) if step else mine)
            out_ref[to, steps * 2 * vocab :] = by_owner(sums, sums)


def head(hidden, weights, meta, norm_gain, steps):
    halves, rows, half = hidden.shape
    vocab = weights[0].shape[1]
    depth = half // 2
    k_blocks = halves * 2
    width = halves * half
    out_shape = (rows // steps * 2, steps * 2 * vocab + 128)
    return pl.pallas_call(
        functools.partial(head_kernel, steps, rows // 4, k_blocks, width),
        grid=(k_blocks,),
        in_specs=[pl.BlockSpec((1, rows, depth), lambda k: (k // 2, 0, k % 2))]
        + [pl.BlockSpec((depth, vocab), lambda k: (k, 0))] * 4
        + [
            pl.BlockSpec(meta.shape, lambda k: (0, 0, 0)),
            pl.BlockSpec((1, depth), lambda k: (0, k)),
        ],
        out_specs=pl.BlockSpec(out_shape, lambda k: (0, 0)),
        out_shape=jax.ShapeDtypeStruct(out_shape, jnp.bfloat16),
        scratch_shapes=[
            pltpu.VMEM((4, rows, vocab), jnp.float32),
            pltpu.VMEM((rows, 128), jnp.float32),
        ],
        compiler_params=pltpu.CompilerParams(vmem_limit_bytes=56 * 1024 * 1024),
        cost_estimate=pl.CostEstimate(
            flops=8 * rows * width * vocab,
            bytes_accessed=2 * (rows * width + 4 * width * vocab),
            transcendentals=4 * rows * vocab,
        ),
        name="logits_and_shard_softmax",
    )(hidden, *weights, meta, norm_gain.reshape(1, -1))


def residual_kernel(parts_ref, residual_ref, gain_ref, out_ref):
    summed = residual_ref[...].astype(jnp.float32)
    for part in range(parts_ref.shape[0]):
        summed = summed + parts_ref[part].astype(jnp.float32)
    out_ref[...] = (summed * gain_ref[...]).astype(jnp.bfloat16)


def add_residual(parts, residual, gain):
    return pl.pallas_call(
        residual_kernel,
        out_shape=jax.ShapeDtypeStruct(residual.shape, jnp.bfloat16),
        compiler_params=pltpu.CompilerParams(vmem_limit_bytes=16 * 1024 * 1024),
        cost_estimate=pl.CostEstimate(
            flops=parts.size, bytes_accessed=2 * parts.size, transcendentals=0
        ),
        name="sum_residual_gain",
    )(parts, residual, gain.reshape(1, -1))


def owner_kernel(tp_count, vocab, place_ref, got_ref, out_ref, stats_ref, offset_ref):
    x = pl.program_id(0)
    cores, rows = got_ref.shape[:2]
    steps = out_ref.shape[0]

    @pl.when(x == 0)
    def _():
        packed = got_ref[:, :, steps * 2 * vocab :].astype(jnp.float32)
        lane = lax.broadcasted_iota(jnp.int32, (1, 1, 128), 2)

        def pieces(start, count):
            mine = jnp.logical_and(lane >= start, lane < start + count)
            return jnp.sum(jnp.where(mine, packed, 0.0), axis=2, keepdims=True)

        for step in range(steps):
            first = step * 10
            peaks, totals = pieces(first, 3), pieces(first + 3, 2)
            moments, targets = pieces(first + 5, 2), pieces(first + 7, 3)
            peak = jnp.max(peaks, axis=0, keepdims=True)
            lift = peaks - peak
            scale = jnp.exp(lift)
            total = jnp.sum(scale * totals, axis=0, keepdims=True)
            moment = jnp.sum(scale * (moments + lift * totals), axis=0, keepdims=True)
            target = jnp.sum(targets, axis=0, keepdims=True)
            log_sum = peak + jnp.log(total)
            entropy = jnp.log(total) - moment / total
            stats = jnp.where(lane == 0, entropy, jnp.where(lane == 1, log_sum - target, 0.0))
            stats_ref[step] = stats[0]
            offset_ref[step] = jnp.broadcast_to(peaks - log_sum, (cores, rows, 128))

    x_low, own_core = place_ref[0], place_ref[1]
    two = lax.rem(x + x_low, 2)
    for shard in range(2):
        core = lax.rem(own_core + shard, 2)
        at_x = lax.rem(x + 4 + two * (2 * core - 1), 4)
        for tp in range(tp_count):
            source = tp * 2 + at_x // 2
            start = pl.multiple_of((core * tp_count + tp) * vocab, vocab)
            for step in range(steps):
                from_column = pl.multiple_of((step * 2 + two) * vocab, vocab)
                values = got_ref[source, :, pl.ds(from_column, vocab)].astype(jnp.float32)
                values = jnp.where(values > 0.0, 0.0, values + offset_ref[step, source][:, :1])
                out_ref[step, :, pl.ds(start, vocab)] = values[shard * 4 : shard * 4 + 4]


def owner(place, got, tp_count, vocab, steps):
    rows = got.shape[1]
    cut = 2 * tp_count * vocab
    return pl.pallas_call(
        functools.partial(owner_kernel, tp_count, vocab),
        grid=(4,),
        in_specs=[
            pl.BlockSpec(memory_space=pltpu.SMEM),
            pl.BlockSpec(got.shape, lambda x: (0, 0, 0)),
        ],
        out_specs=[
            pl.BlockSpec((steps, 4, cut), lambda x: (0, 0, x)),
            pl.BlockSpec((steps, rows, 128), lambda x: (0, 0, 0)),
        ],
        out_shape=[
            jax.ShapeDtypeStruct((steps, 4, 4 * cut), jnp.float32),
            jax.ShapeDtypeStruct((steps, rows, 128), jnp.float32),
        ],
        scratch_shapes=[pltpu.VMEM((steps, 2 * tp_count, rows, 128), jnp.float32)],
        compiler_params=pltpu.CompilerParams(vmem_limit_bytes=32 * 1024 * 1024),
        cost_estimate=pl.CostEstimate(
            flops=8 * steps * rows * cut, bytes_accessed=12 * steps * rows * cut, transcendentals=0
        ),
        name="owned_log_probs",
    )(place, got)


def body(
    queries,
    latent_cache,
    new_latent,
    lengths,
    value_up_weight,
    out_proj,
    residual,
    norm_gain,
    head_weight,
    mask_bits,
    targets,
):
    rows, steps = queries.shape[:2]
    width = residual.shape[2]
    half = width // 2
    vocab_dev = head_weight.shape[1]
    tp_count, groups = lax.axis_size(TP), lax.axis_size(TP) // 2
    group_rows = rows // groups
    pairs = steps * group_rows
    x_high, x_low, core = (lax.axis_index(axis) for axis in DP)
    x, tp = 2 * x_high + x_low, lax.axis_index(TP)

    def other_core(value):
        return lax.ppermute(value, "core", ((0, 1), (1, 0)))

    def next_chip(value):
        return lax.ppermute(
            value, DP, tuple(((i + 2 - 4 * (i % 2)) % 8, i) for i in range(8))
        )

    def four(own):
        near = next_chip(own)
        return [own, other_core(own), near, other_core(near)]

    weights = four(head_weight)
    shard_x = jnp.stack([x, x, x + 1 - 2 * core, x - 1 + 2 * core]) % 4
    shard = (2 * shard_x + jnp.stack([core, 1 - core, core, 1 - core])) * tp_count + tp

    def rows_here(full):
        cut = full.reshape(2, 2, 2, groups, group_rows, steps)
        cut = lax.dynamic_slice(
            cut, (0, x_low, core, 0, 0, 0), (2, 1, 1, groups, group_rows, steps)
        )
        return cut.reshape(2, groups, group_rows, steps).transpose(1, 0, 3, 2).reshape(-1)

    words = [rows_here(one) for one in four(mask_bits.reshape(-1, steps))]
    local_targets = rows_here(targets) - (shard * vocab_dev)[:, None]
    meta = jnp.concatenate([jnp.stack(words), local_targets])[..., None]

    partial = attention(
        queries, latent_cache, new_latent, lengths, value_up_weight, out_proj
    )
    own_half, own_group = tp // groups, tp % groups
    resid = lax.dynamic_slice(
        residual.transpose(1, 0, 2),
        (0, own_group * group_rows, own_half * half),
        (steps, group_rows, half),
    ).reshape(pairs, half)
    gain = lax.dynamic_slice_in_dim(norm_gain, own_half * half, half, 0)
    attn = lax.all_to_all(
        partial.reshape(tp_count, pairs, half), TP, split_axis=0, concat_axis=0, tiled=True
    )
    hidden = add_residual(attn, resid, gain)
    across = lax.ppermute(hidden, "xh", ((0, 1), (1, 0)))
    hidden = jnp.where(x_high == 0, jnp.stack([hidden, across]), jnp.stack([across, hidden]))
    hidden = lax.all_gather(hidden, TP, axis=0).reshape(2, groups * 2 * pairs, half)
    sent = head(hidden, weights, meta, norm_gain, steps)
    sent = sent.reshape(tp_count * 2, 8, -1)
    sent = lax.all_to_all(sent, ("z", "y", "xh"), split_axis=0, concat_axis=0, tiled=True)
    log_probs, stats = owner(jnp.stack([x_low, core]), sent, tp_count, vocab_dev, steps)
    own_rows = rows // tp_count
    entropy = stats[:, :own_rows, 0].T
    row_loss = jnp.mean(stats[:, :own_rows, 1], axis=0)
    return (log_probs.transpose(1, 0, 2), entropy, row_loss)


def solution(mesh):
    axes = DP + TP
    mesh = jax.sharding.Mesh(mesh.devices.reshape(2, 2, 2, 4, 4), axes)
    placed = (
        P(DP, None, TP, None),
        P(DP, None, None),
        P(DP, None, None),
        P(DP),
        P(TP, None, None),
        P(TP, None),
        P(DP, None, None),
        P(),
        P(None, axes),
        P(None, None, axes),
        P(),
    )
    return jax.shard_map(
        body,
        mesh=mesh,
        in_specs=placed,
        out_specs=(P(axes, None, None), P(axes, None), P(axes)),
        check_vma=False,
    )
```

```python
import functools

import jax
import jax.numpy as jnp
from jax import lax
from jax.experimental import pallas as pl
from jax.experimental.pallas import tpu as pltpu
from jax.sharding import PartitionSpec as P

LAT = 512
DP = ("xh", "xl", "core")
TP = ("z", "y")


score_scale = 192.0 ** (-0.5)
neg_large = -1e30


def attend(lengths, queries_ref, cache_ref, new_ref, up_ref, start, count):
    context = cache_ref.shape[2]
    steps, heads = queries_ref.shape[1:3]
    value = up_ref.shape[2]
    tall = count * 16
    position = lax.broadcasted_iota(jnp.int32, (1, context), 1)
    blank = jnp.zeros((heads, queries_ref.shape[3]), jnp.float32)
    lines = []
    for row in range(start, start + count):
        parts = [queries_ref[row, step].astype(jnp.float32) for step in range(steps)]
        lines.append(jnp.concatenate(parts + [blank], axis=0).astype(jnp.bfloat16))
    latents = jnp.concatenate(
        [new_ref[place].astype(jnp.float32)[start : start + count] for place in range(steps)], axis=0
    ).astype(jnp.bfloat16)
    scores = []
    for row in range(count):
        one = jnp.dot(lines[row], cache_ref[start + row], preferred_element_type=jnp.float32)
        scores.append(jnp.where(position < lengths[row], one * score_scale, neg_large))
    scores = jnp.concatenate(scores, axis=0)
    fresh = lax.dot_general(
        jnp.concatenate(lines, axis=0),
        latents,
        (((1,), (1,)), ((), ())),
        preferred_element_type=jnp.float32,
    )
    line = lax.broadcasted_iota(jnp.int32, fresh.shape, 0)
    key = lax.broadcasted_iota(jnp.int32, fresh.shape, 1)
    step = (line % 16) // 4
    own = jnp.logical_and(line // 16 == key % count, key // count <= step)
    fresh = jnp.where(own, fresh * score_scale, neg_large)
    top = jnp.maximum(
        jnp.max(scores, axis=1, keepdims=True), jnp.max(fresh, axis=1, keepdims=True)
    )
    scores = jnp.exp(scores - top)
    fresh = jnp.exp(fresh - top)
    denom = jnp.sum(scores, axis=1, keepdims=True) + jnp.sum(fresh, axis=1, keepdims=True)
    scores = (scores / denom).astype(jnp.bfloat16)
    fresh = (fresh / denom).astype(jnp.bfloat16)
    latent = []
    for row in range(count):
        latent.append(
            lax.dot_general(
                scores[row * 16 : row * 16 + 16],
                cache_ref[start + row, :LAT, :],
                (((1,), (1,)), ((), ())),
                preferred_element_type=jnp.float32,
            )
        )
    latent = jnp.concatenate(latent, axis=0) + jnp.dot(
        fresh, latents[:, :LAT], preferred_element_type=jnp.float32
    )
    latent = latent.astype(jnp.bfloat16)
    values = jnp.concatenate(
        [jnp.dot(latent, up_ref[head], preferred_element_type=jnp.float32) for head in range(heads)],
        axis=1,
    )
    line = lax.broadcasted_iota(jnp.int32, values.shape, 0)
    entry = lax.broadcasted_iota(jnp.int32, values.shape, 1)
    values = jnp.where(line % 4 == entry // value, values, 0.0).astype(jnp.bfloat16)
    shape = (steps * count, tall)
    target = lax.broadcasted_iota(jnp.int32, shape, 0)
    line = lax.broadcasted_iota(jnp.int32, shape, 1)
    pick = jnp.logical_and(target % count == line // 16, target // count == (line % 16) // 4)
    pick = jnp.where(pick, 1.0, 0.0).astype(jnp.bfloat16)
    return jnp.dot(pick, values, preferred_element_type=jnp.float32)


def attention_kernel(
    lengths_ref,
    queries_ref,
    cache_ref,
    new_ref,
    up_ref,
    project_ref,
    head_ref,
    out_ref,
    first_ref,
    second_ref,
    values_ref,
    weight_ref,
    sems,
):
    g = pl.program_id(0)
    parts = sems.shape[0]
    depth = weight_ref.shape[0] // parts
    copies = [
        pltpu.make_async_copy(
            project_ref.at[pl.ds(part * depth, depth)],
            weight_ref.at[pl.ds(part * depth, depth)],
            sems.at[part],
        )
        for part in range(parts)
    ]
    @pl.when(g == 0)
    def _():
        for copy in copies:
            copy.start()

    middle = pl.num_programs(0) // 2

    @pl.when(g < middle)
    def _():
        first_ref[...] = head_ref[...]

    @pl.when(g >= middle)
    def _():
        second_ref[...] = head_ref[...]

    count = 8
    block = cache_ref.shape[0]
    lengths = [lengths_ref[g * block + row] for row in range(block)]
    values = [
        attend(lengths[start : start + count], queries_ref, cache_ref, new_ref, up_ref, start, count)
        for start in range(0, block, count)
    ]
    values = jnp.concatenate(values, axis=0).astype(jnp.bfloat16)
    lines = values.shape[0]
    values_ref[pl.ds(pl.multiple_of(g * lines, lines), lines), :] = values

    @pl.when(g == pl.num_programs(0) - 1)
    def _():
        for copy in copies:
            copy.wait()
        half = out_ref.shape[2]
        cut = half // 4
        for part in range(8):
            columns = slice((part % 4) * cut, (part % 4 + 1) * cut)
            out_ref[part // 4, :, columns] = jnp.dot(
                values_ref[...],
                weight_ref[:, part * cut : (part + 1) * cut],
                preferred_element_type=jnp.float32,
            ).astype(jnp.bfloat16)


def attention(queries, latent_cache, new_latent, lengths, value_up_weight, out_proj, head_weight):
    rows, steps, heads, entries = queries.shape
    context = latent_cache.shape[1]
    block = 16
    grid = rows // block
    depth, width = out_proj.shape
    head_block = (width // grid, head_weight.shape[1])
    return pl.pallas_call(
        attention_kernel,
        grid_spec=pltpu.PrefetchScalarGridSpec(
            num_scalar_prefetch=1,
            grid=(grid,),
            in_specs=[
                pl.BlockSpec((block, steps, heads, entries), lambda g, _: (g, 0, 0, 0)),
                pl.BlockSpec((block, entries, context), lambda g, _: (g, 0, 0)),
                pl.BlockSpec((steps, block, entries), lambda g, _: (0, g, 0)),
                pl.BlockSpec(value_up_weight.shape, lambda g, _: (0, 0, 0)),
                pl.BlockSpec(memory_space=pl.ANY),
                pl.BlockSpec(head_block, lambda g, _: (g, 0)),
            ],
            out_specs=[
                pl.BlockSpec((2, rows * steps, width // 2), lambda g, _: (0, 0, 0)),
                pl.BlockSpec(head_block, lambda g, _: (jnp.minimum(g, grid // 2 - 1), 0)),
                pl.BlockSpec(head_block, lambda g, _: (jnp.maximum(g - grid // 2, 0), 0)),
            ],
            scratch_shapes=[
                pltpu.VMEM((rows * steps, depth), jnp.bfloat16),
                pltpu.VMEM((depth, width), jnp.bfloat16),
                pltpu.SemaphoreType.DMA((4,)),
            ],
        ),
        out_shape=[
            jax.ShapeDtypeStruct((2, rows * steps, width // 2), jnp.bfloat16),
        ]
        + [jax.ShapeDtypeStruct((width // 2, head_weight.shape[1]), jnp.bfloat16)] * 2,
        compiler_params=pltpu.CompilerParams(vmem_limit_bytes=56 * 1024 * 1024),
        cost_estimate=pl.CostEstimate(
            flops=4 * rows * 16 * context * entries + 2 * rows * steps * depth * width,
            bytes_accessed=2 * rows * context * entries + 2 * depth * width,
            transcendentals=rows * 16 * context,
        ),
        name="latent_attention",
    )(
        lengths,
        queries,
        latent_cache.transpose(0, 2, 1),
        new_latent.transpose(1, 0, 2),
        value_up_weight,
        out_proj,
        head_weight,
    )


def nothing_kernel(value_ref, after_ref, out_ref):
    pass


def once(value, after):
    anywhere = pl.BlockSpec(memory_space=pl.ANY)
    return pl.pallas_call(
        nothing_kernel,
        in_specs=[anywhere, anywhere],
        out_specs=anywhere,
        out_shape=jax.ShapeDtypeStruct(value.shape, value.dtype),
        input_output_aliases={0: 0},
        name="value_after",
    )(value, after)


def head_kernel(steps, per_block, k_blocks, width, a_ref, *refs):
    weight_refs = refs[:2]
    moved_refs = refs[2:6]
    meta_ref, gain_ref, out_ref, acc_ref, squares_ref = refs[6:]
    k = pl.program_id(0)

    @pl.when(k == 0)
    def _():
        acc_ref[...] = jnp.zeros_like(acc_ref)
        squares_ref[...] = jnp.zeros_like(squares_ref)

    rows, depth = a_ref.shape[1:]
    vocab = weight_refs[0].shape[1]
    a = a_ref[0]
    for shard, weight_ref in enumerate(weight_refs):
        acc_ref[shard] += jnp.dot(a, weight_ref[...], preferred_element_type=jnp.float32)
    for part in range(2):

        @pl.when(k // (k_blocks // 2) == part)
        def _(part=part):
            for shard in range(2):
                weight_ref = moved_refs[2 * shard + part]
                acc_ref[2 + shard] += jnp.dot(
                    a, weight_ref[...], preferred_element_type=jnp.float32
                )

    inverse = 1.0 / gain_ref[...]
    wide = a.astype(jnp.float32) * inverse
    wide = wide * wide
    part = wide[:, :128]
    for lane in range(128, depth, 128):
        part = part + wide[:, lane : lane + 128]
    squares_ref[...] += part

    @pl.when(k == k_blocks - 1)
    def _():
        column = lax.broadcasted_iota(jnp.int32, (1, vocab), 1)
        bit = column // (vocab // 16)
        lane = lax.broadcasted_iota(jnp.int32, (1, 128), 1)
        upper = lax.broadcasted_iota(jnp.int32, (1, 8, 1), 1) < 4

        def of_step(full, step):
            return full.reshape(-1, steps, 8, full.shape[1])[:, step]

        def by_owner(first, second):
            count = first.shape[2]
            low = jnp.where(upper, first, pltpu.roll(second, 4, 1))
            high = jnp.where(upper, pltpu.roll(first, 4, 1), second)
            low, high = (one.reshape(-1, 2, 8, count) for one in (low, high))
            return jnp.stack([low, high], axis=1).reshape(-1, count).astype(jnp.bfloat16)

        for block in range(rows // per_block):
            own = pl.ds(block * per_block, per_block)
            to = pl.ds(block * (per_block // steps * 2), per_block // steps * 2)
            square = jnp.sum(squares_ref[own, :], axis=1, keepdims=True)
            norm = lax.rsqrt(square * (1.0 / width) + 1e-06)
            logits, allowed, target, peak = [], [], 0.0, neg_large
            for shard in range(4):
                one = acc_ref[shard, own, :] * norm
                word = meta_ref[shard, own, :]
                is_target = column == meta_ref[4 + shard, own, :]
                open_bit = jnp.bitwise_and(jnp.right_shift(word, bit), 1) == 1
                ok = jnp.logical_or(open_bit, is_target)
                logits.append(one)
                allowed.append(ok)
                target = target + jnp.where(is_target, one, 0.0)
                peak = jnp.maximum(peak, jnp.where(ok, one, neg_large))
            target = jnp.sum(target, axis=1, keepdims=True)
            peak = jnp.max(peak, axis=1, keepdims=True)
            total, moment, sent = 0.0, 0.0, []
            for ok, one in zip(allowed, logits):
                shifted = jnp.where(ok, one - peak, 0.0)
                weight = jnp.where(ok, jnp.exp(shifted), 0.0)
                total = total + weight
                moment = moment + weight * shifted
                sent.append(jnp.where(ok, shifted, 1.0))
            total = jnp.sum(total, axis=1, keepdims=True)
            moment = jnp.sum(moment, axis=1, keepdims=True)
            packed = jnp.zeros((per_block, 128), jnp.float32)
            lanes = 0
            for stat, count in ((peak, 3), (total, 2), (moment, 2), (target, 3)):
                for _ in range(count):
                    piece = stat.astype(jnp.bfloat16).astype(jnp.float32)
                    packed = jnp.where(lane == lanes, piece, packed)
                    stat = stat - piece
                    lanes += 1
            sums = 0.0
            for step in range(steps):
                for two in range(2):
                    start = (step * 2 + two) * vocab
                    out_ref[to, start : start + vocab] = by_owner(
                        of_step(sent[2 * two], step), of_step(sent[2 * two + 1], step)
                    )
                mine = of_step(packed, step)
                sums = sums + (pltpu.roll(mine, step * lanes, 2) if step else mine)
            out_ref[to, steps * 2 * vocab :] = by_owner(sums, sums)


def head(hidden, weights, meta, norm_gain, steps):
    halves, rows, half = hidden.shape
    vocab = weights[0].shape[1]
    depth = half // 2
    k_blocks = halves * 2
    width = halves * half
    out_shape = (rows // steps * 2, steps * 2 * vocab + 128)
    return pl.pallas_call(
        functools.partial(head_kernel, steps, rows // 4, k_blocks, width),
        grid=(k_blocks,),
        in_specs=[pl.BlockSpec((1, rows, depth), lambda k: (k // 2, 0, k % 2))]
        + [pl.BlockSpec((depth, vocab), lambda k: (k, 0))] * 2
        + [
            pl.BlockSpec((depth, vocab), lambda k: (jnp.minimum(k, k_blocks // 2 - 1), 0)),
            pl.BlockSpec((depth, vocab), lambda k: (jnp.maximum(k - k_blocks // 2, 0), 0)),
        ]
        * 2
        + [
            pl.BlockSpec(meta.shape, lambda k: (0, 0, 0)),
            pl.BlockSpec((1, depth), lambda k: (0, k)),
        ],
        out_specs=pl.BlockSpec(out_shape, lambda k: (0, 0)),
        out_shape=jax.ShapeDtypeStruct(out_shape, jnp.bfloat16),
        scratch_shapes=[
            pltpu.VMEM((4, rows, vocab), jnp.float32),
            pltpu.VMEM((rows, 128), jnp.float32),
        ],
        compiler_params=pltpu.CompilerParams(vmem_limit_bytes=56 * 1024 * 1024),
        cost_estimate=pl.CostEstimate(
            flops=8 * rows * width * vocab,
            bytes_accessed=2 * (rows * width + 4 * width * vocab),
            transcendentals=4 * rows * vocab,
        ),
        name="logits_and_shard_softmax",
    )(hidden, *weights, meta, norm_gain.reshape(1, -1))


def residual_kernel(parts_ref, residual_ref, gain_ref, after_ref, out_ref):
    summed = residual_ref[...].astype(jnp.float32)
    for part in range(parts_ref.shape[0]):
        summed = summed + parts_ref[part].astype(jnp.float32)
    out_ref[...] = (summed * gain_ref[...]).astype(jnp.bfloat16)


def add_residual(parts, residual, gain, after):
    in_vmem = pl.BlockSpec(memory_space=pltpu.VMEM)
    return pl.pallas_call(
        residual_kernel,
        in_specs=[in_vmem, in_vmem, in_vmem, pl.BlockSpec(memory_space=pl.ANY)],
        out_specs=in_vmem,
        out_shape=jax.ShapeDtypeStruct(residual.shape, jnp.bfloat16),
        compiler_params=pltpu.CompilerParams(vmem_limit_bytes=16 * 1024 * 1024),
        cost_estimate=pl.CostEstimate(
            flops=parts.size, bytes_accessed=2 * parts.size, transcendentals=0
        ),
        name="sum_residual_gain",
    )(parts, residual, gain.reshape(1, -1), after)


def owner_kernel(tp_count, vocab, place_ref, got_ref, out_ref, stats_ref, offset_ref):
    x = pl.program_id(0)
    cores, rows = got_ref.shape[:2]
    steps = out_ref.shape[0]

    @pl.when(x == 0)
    def _():
        packed = got_ref[:, :, steps * 2 * vocab :].astype(jnp.float32)
        lane = lax.broadcasted_iota(jnp.int32, (1, 1, 128), 2)

        def pieces(start, count):
            mine = jnp.logical_and(lane >= start, lane < start + count)
            return jnp.sum(jnp.where(mine, packed, 0.0), axis=2, keepdims=True)

        for step in range(steps):
            first = step * 10
            peaks, totals = pieces(first, 3), pieces(first + 3, 2)
            moments, targets = pieces(first + 5, 2), pieces(first + 7, 3)
            peak = jnp.max(peaks, axis=0, keepdims=True)
            lift = peaks - peak
            scale = jnp.exp(lift)
            total = jnp.sum(scale * totals, axis=0, keepdims=True)
            moment = jnp.sum(scale * (moments + lift * totals), axis=0, keepdims=True)
            target = jnp.sum(targets, axis=0, keepdims=True)
            log_sum = peak + jnp.log(total)
            entropy = jnp.log(total) - moment / total
            stats = jnp.where(lane == 0, entropy, jnp.where(lane == 1, log_sum - target, 0.0))
            stats_ref[step] = stats[0]
            offset_ref[step] = jnp.broadcast_to(peaks - log_sum, (cores, rows, 128))

    x_low, own_core = place_ref[0], place_ref[1]
    two = lax.rem(x + x_low, 2)
    for shard in range(2):
        core = lax.rem(own_core + shard, 2)
        at_x = lax.rem(x + 4 + two * (2 * core - 1), 4)
        for tp in range(tp_count):
            source = tp * 2 + at_x // 2
            start = pl.multiple_of((core * tp_count + tp) * vocab, vocab)
            for step in range(steps):
                from_column = pl.multiple_of((step * 2 + two) * vocab, vocab)
                values = got_ref[source, :, pl.ds(from_column, vocab)].astype(jnp.float32)
                values = jnp.where(values > 0.0, 0.0, values + offset_ref[step, source][:, :1])
                out_ref[step, :, pl.ds(start, vocab)] = values[shard * 4 : shard * 4 + 4]


def owner(place, got, tp_count, vocab, steps):
    rows = got.shape[1]
    cut = 2 * tp_count * vocab
    return pl.pallas_call(
        functools.partial(owner_kernel, tp_count, vocab),
        grid=(4,),
        in_specs=[
            pl.BlockSpec(memory_space=pltpu.SMEM),
            pl.BlockSpec(got.shape, lambda x: (0, 0, 0)),
        ],
        out_specs=[
            pl.BlockSpec((steps, 4, cut), lambda x: (0, 0, x)),
            pl.BlockSpec((steps, rows, 128), lambda x: (0, 0, 0)),
        ],
        out_shape=[
            jax.ShapeDtypeStruct((steps, 4, 4 * cut), jnp.float32),
            jax.ShapeDtypeStruct((steps, rows, 128), jnp.float32),
        ],
        scratch_shapes=[pltpu.VMEM((steps, 2 * tp_count, rows, 128), jnp.float32)],
        compiler_params=pltpu.CompilerParams(vmem_limit_bytes=32 * 1024 * 1024),
        cost_estimate=pl.CostEstimate(
            flops=8 * steps * rows * cut, bytes_accessed=12 * steps * rows * cut, transcendentals=0
        ),
        name="owned_log_probs",
    )(place, got)


def body(
    queries,
    latent_cache,
    new_latent,
    lengths,
    value_up_weight,
    out_proj,
    residual,
    norm_gain,
    head_weight,
    mask_bits,
    targets,
):
    rows, steps = queries.shape[:2]
    width = residual.shape[2]
    half = width // 2
    vocab_dev = head_weight.shape[1]
    tp_count, groups = lax.axis_size(TP), lax.axis_size(TP) // 2
    group_rows = rows // groups
    pairs = steps * group_rows
    x_high, x_low, core = (lax.axis_index(axis) for axis in DP)
    x, tp = 2 * x_high + x_low, lax.axis_index(TP)

    def other_core(value):
        return lax.ppermute(value, "core", ((0, 1), (1, 0)))

    def next_chip(value):
        return lax.ppermute(
            value, DP, tuple(((i + 2 - 4 * (i % 2)) % 8, i) for i in range(8))
        )

    def four(own):
        near = next_chip(own)
        return [own, other_core(own), near, other_core(near)]

    shard_x = jnp.stack([x, x, x + 1 - 2 * core, x - 1 + 2 * core]) % 4
    shard = (2 * shard_x + jnp.stack([core, 1 - core, core, 1 - core])) * tp_count + tp

    def rows_here(full):
        cut = full.reshape(2, 2, 2, groups, group_rows, steps)
        cut = lax.dynamic_slice(
            cut, (0, x_low, core, 0, 0, 0), (2, 1, 1, groups, group_rows, steps)
        )
        return cut.reshape(2, groups, group_rows, steps).transpose(1, 0, 3, 2).reshape(-1)

    words = [rows_here(one) for one in four(mask_bits.reshape(-1, steps))]
    local_targets = rows_here(targets) - (shard * vocab_dev)[:, None]
    meta = jnp.concatenate([jnp.stack(words), local_targets])[..., None]

    partial, first_half, second_half = attention(
        queries, latent_cache, new_latent, lengths, value_up_weight, out_proj, head_weight
    )
    own_half, own_group = tp // groups, tp % groups
    resid = lax.dynamic_slice(
        residual.transpose(1, 0, 2),
        (0, own_group * group_rows, own_half * half),
        (steps, group_rows, half),
    ).reshape(pairs, half)
    gain = lax.dynamic_slice_in_dim(norm_gain, own_half * half, half, 0)
    attn = lax.all_to_all(
        partial.reshape(tp_count, pairs, half), TP, split_axis=0, concat_axis=0, tiled=True
    )
    near = next_chip(first_half)
    hidden = add_residual(attn, resid, gain, near)
    across = lax.ppermute(hidden, "xh", ((0, 1), (1, 0)))
    hidden = jnp.where(x_high == 0, jnp.stack([hidden, across]), jnp.stack([across, hidden]))
    near = [near, next_chip(once(second_half, hidden))]
    weights = [head_weight, other_core(head_weight)] + near + [other_core(one) for one in near]
    hidden = lax.all_gather(hidden, TP, axis=0).reshape(2, groups * 2 * pairs, half)
    sent = head(hidden, weights, meta, norm_gain, steps)
    sent = sent.reshape(tp_count * 2, 8, -1)
    sent = lax.all_to_all(sent, ("z", "y", "xh"), split_axis=0, concat_axis=0, tiled=True)
    log_probs, stats = owner(jnp.stack([x_low, core]), sent, tp_count, vocab_dev, steps)
    own_rows = rows // tp_count
    entropy = stats[:, :own_rows, 0].T
    row_loss = jnp.mean(stats[:, :own_rows, 1], axis=0)
    return (log_probs.transpose(1, 0, 2), entropy, row_loss)


def solution(mesh):
    axes = DP + TP
    mesh = jax.sharding.Mesh(mesh.devices.reshape(2, 2, 2, 4, 4), axes)
    placed = (
        P(DP, None, TP, None),
        P(DP, None, None),
        P(DP, None, None),
        P(DP),
        P(TP, None, None),
        P(TP, None),
        P(DP, None, None),
        P(),
        P(None, axes),
        P(None, None, axes),
        P(),
    )
    return jax.shard_map(
        body,
        mesh=mesh,
        in_specs=placed,
        out_specs=(P(axes, None, None), P(axes, None), P(axes)),
        check_vma=False,
    )
```
